32 devices in a mesh: row: 4 (over x, core), col: 8 (over z, y).
Axes of the slice: x: 2, y: 2, z: 4, core: 2. Of those that a mesh axis runs over, the one named last changes fastest.
Arguments:
- features: float32 [3, 4, 512, 768], P(None, 'row'), may hold values from -6 to 6
- ridge: float32 [3, 4, 512], P(None, 'row'), may hold values from 0.5 to 4
Outputs:
- schur: float32 [3, 4, 512, 6, 8, 128], P(None, 'row', None, None, 'col')
- panel: float32 [3, 4, 512, 512], P(None, 'row')
The draws below stay inside these ranges and needn't reach their ends.
All inputs are finite; a program needn't handle non-finite values.
Results may differ from the reference program's by a relative error of at most 0.00017.
Values sent between devices are 32-bit elements; how exact they have to be, the bound alone decides.
A program may use at most 64 MiB of HBM per device.

```python
import math
import jax
import jax.numpy as jnp
from jax import lax

F = 768
B = 512
CB = 128
RT = 3
CT = 6
N_ROW = 4
N_COL = 8


def steps_of(stream_key, extent, shards, least, high):
    gain = 1.0
    for position, parts in shards:
        draws = jax.random.uniform(jax.random.fold_in(jax.random.fold_in(stream_key, 6), position), (parts,), jnp.float32, least / len(shards), high / len(shards))
        gain = gain * jnp.repeat(jnp.exp(draws), extent[position] // parts).reshape((-1,) + (1,) * (len(extent) - 1 - position))
    return gain


def normal_values(key, shape, deviation, most, shards=(), kind=jnp.bfloat16):
    loudness = steps_of(key, shape, shards, -0.22, 0.18) if shards else 1.0
    entries = jax.random.normal(key, shape, jnp.float32) * deviation * loudness
    return jnp.minimum(jnp.maximum(entries, -most), most).astype(kind)


def setup_inputs(seed: int = 0) -> dict:
    streams_of = jax.random.split(jax.random.key(seed), 3)
    features = normal_values(streams_of[0], (RT, N_ROW, B, F), 1.0, 6.0, ((1, 4),), jnp.float32)
    ridge = jnp.clip(jnp.exp(math.log(4.0) - 2.0794415 * jax.random.uniform(streams_of[1], (RT, N_ROW, B), jnp.float32) ** steps_of(streams_of[1], (RT, N_ROW, B), ((1, 4),), -0.2, 0.2)), 0.5, 4.0)
    return dict(features=features, ridge=ridge)


def kernel_of(left, right):
    inner = jnp.dot(left.astype(jnp.float32), right.T.astype(jnp.float32), precision=lax.Precision.HIGHEST, preferred_element_type=jnp.float32)
    return jnp.square(inner / F + 1.0)

def reference(features, ridge):
    samples = features.reshape(-1, F)
    ridge_all = ridge.reshape(-1)
    count = samples.shape[0]
    panel_feat = samples[:B]
    block = kernel_of(panel_feat, panel_feat) + jnp.diag(ridge_all[:B])
    lower = jnp.linalg.cholesky(block)
    match = jnp.arange(count, dtype=jnp.int32)[:, None] == jnp.arange(B, dtype=jnp.int32)[None, :]
    kp_block = kernel_of(samples, panel_feat) + jnp.where(match, ridge_all[:B][None, :], jnp.float32(0.0))
    panel = jax.scipy.linalg.solve_triangular(lower, kp_block.T, lower=True).T
    whole = kernel_of(samples, samples) + jnp.diag(ridge_all)
    schur = whole - jnp.dot(panel.astype(jnp.float32), panel.T.astype(jnp.float32), precision=lax.Precision.HIGHEST, preferred_element_type=jnp.float32)
    return (schur.reshape(RT, N_ROW, B, CT, N_COL, CB), panel.reshape(RT, N_ROW, B, B))
```

```python
import functools

import jax
import jax.numpy as jnp
from jax import lax
from jax.experimental import pallas as pl
from jax.experimental.pallas import tpu as pltpu
from jax.sharding import PartitionSpec as P

CB = 128
STEP = 4
HIGHEST = lax.Precision.HIGHEST
MESH = pl.DeviceIdType.MESH


def dot_t(a, b, precision=None):
    return lax.dot_general(
        a, b, (((1,), (1,)), ((), ())), precision=precision, preferred_element_type=jnp.float32
    )


def split(x):
    hi = x.astype(jnp.bfloat16)
    return hi, (x - hi.astype(jnp.float32)).astype(jnp.bfloat16)


def dot3_t(a, b):
    return dot_t(a[0], b[0]) + (dot_t(a[0], b[1]) + dot_t(a[1], b[0]))


def kernel_value(inner, width):
    return jnp.square(inner * (1.0 / width) + 1.0)


def factor_inverse(w):
    n = w.shape[0]
    lanes = lax.broadcasted_iota(jnp.int32, (1, n), 1)
    rows_out = []
    for j in range(0, n, STEP):
        top = j // 8 * 8
        if w.shape[0] != n - top:
            w = w[8:, :]
        at = j - top
        ids = top + lax.broadcasted_iota(jnp.int32, w.shape, 0)
        all_lanes = lax.broadcasted_iota(jnp.int32, w.shape, 1)
        cols = [jnp.broadcast_to(w[:, j + k : j + k + 1], w.shape) for k in range(STEP)]
        inside = (all_lanes >= j) & (all_lanes < j + STEP) & (ids >= j)
        w = jnp.where(inside, jnp.where(ids == all_lanes, 1.0, 0.0), w)
        rows = [w[at + k : at + k + 1, :] for k in range(STEP)]
        for k in range(STEP):
            piv = cols[k][at + k : at + k + 1, :]
            inv = 1.0 / piv
            scaled = rows[k] * inv
            for m in range(k + 1, STEP):
                rows[m] = rows[m] - cols[k][at + m : at + m + 1, :] * scaled
                cols[m] = cols[m] - cols[k] * (cols[m][at + k : at + k + 1, :] * inv)
            w = w - jnp.where(ids > j + k, cols[k], 0.0) * scaled
            rows_out.append(jnp.where(lanes <= j + k, rows[k] * lax.rsqrt(piv), 0.0))
    return jnp.concatenate(rows_out, axis=0)


def factor_kernel(
    shape, n_row, n_col, feat, ridge0, linv, buf, ridge_p, kp_s,
    local_sem, send_sem, relay_sem, recv_sem, ridge_send, ridge_recv,
):
    width, depth, chunks, slots = shape
    r = lax.axis_index("row")
    q = lax.axis_index("col")
    mate = r + 1 - 2 * (r % 2)
    parity = r % 2
    pair = r // 2
    n_pair = n_row // 2

    barrier = pltpu.get_barrier_semaphore()
    for d in range(1, n_row):
        pl.semaphore_signal(
            barrier, inc=1, device_id=(lax.rem(r + d, n_row), q), device_id_type=MESH
        )
    pl.semaphore_wait(barrier, n_row - 1)

    def place(u):
        if u < chunks:
            return 0, 0, u * CB
        first = ((u - chunks) * n_col + q) * CB
        tile = first // width
        return tile % n_row, tile // n_row, first % width

    def source(u):
        owner, tile, off = place(u)
        return feat.at[tile, pl.ds(pl.multiple_of(off, CB), CB), :]

    def dest(u):
        return buf.at[pl.ds(u * CB, CB), :]

    def send(u, d):
        to = mate if d == 0 else 2 * lax.rem(pair + d, n_pair) + parity
        return pltpu.make_async_remote_copy(
            src_ref=source(u), dst_ref=dest(u), send_sem=send_sem.at[u, d],
            recv_sem=recv_sem.at[u], device_id=(to, q), device_id_type=MESH,
        )

    def forward(u):
        return pltpu.make_async_remote_copy(
            src_ref=dest(u), dst_ref=dest(u), send_sem=relay_sem.at[u],
            recv_sem=recv_sem.at[u], device_id=(mate, q), device_id_type=MESH,
        )

    def own(u):
        return pltpu.make_async_copy(source(u), dest(u), local_sem.at[u])

    def start(u):
        @pl.when(place(u)[0] == r)
        def _():
            for d in range(1, n_pair):
                send(u, d).start()
            send(u, 0).start()
            own(u).start()

    def is_relay(u):
        owner = place(u)[0]
        return (owner != r) & (owner % 2 == parity)

    def arrive(u):
        @pl.when(place(u)[0] == r)
        def _():
            own(u).wait()

        @pl.when(place(u)[0] != r)
        def _():
            forward(u).wait_recv()

        @pl.when(is_relay(u))
        def _():
            forward(u).start()

    def finish(u):
        @pl.when(place(u)[0] == r)
        def _():
            for d in range(n_pair):
                send(u, d).wait_send()

        @pl.when(is_relay(u))
        def _():
            forward(u).wait_send()

    def ridge_copy(d):
        return pltpu.make_async_remote_copy(
            src_ref=ridge0, dst_ref=ridge_p, send_sem=ridge_send.at[d], recv_sem=ridge_recv,
            device_id=(lax.rem(r + d, n_row), q), device_id_type=MESH,
        )

    @pl.when(r == 0)
    def _():
        for d in range(1, n_row):
            ridge_copy(d).start()
        ridge_p[...] = ridge0[...]

    for u in range(chunks):
        start(u)

    @pl.when(r != 0)
    def _():
        ridge_copy(1).wait_recv()

    linv[...] = jnp.zeros_like(linv)
    late = chunks + (slots + 1) // 2
    for p in range(chunks):
        arrive(p)
        if p == 0:
            for u in range(chunks, chunks + slots):
                start(u)
        if p == chunks - 1:
            for u in range(chunks, late):
                arrive(u)
        here = slice(p * CB, (p + 1) * CB)
        upto = (p + 1) * CB
        mine = buf[here, :]
        for c in range(p + 1):
            there = slice(c * CB, (c + 1) * CB)
            kp_s[p % 2, :, there] = kernel_value(dot_t(mine, buf[there, :], HIGHEST), depth)
        eye = lax.broadcasted_iota(jnp.int32, (CB, CB), 0) == lax.broadcasted_iota(
            jnp.int32, (CB, CB), 1
        )
        s = kp_s[p % 2, :, here] + jnp.where(eye, ridge_p[:, here], 0.0)
        if p > 0:
            before = linv[0 : p * CB, 0 : p * CB]
            low = dot_t(kp_s[p % 2, :, 0 : p * CB], before, HIGHEST)
            s = s - dot_t(low, low, HIGHEST)
            across = jnp.dot(low, before, precision=HIGHEST, preferred_element_type=jnp.float32)
        inv = factor_inverse(s)
        linv[here, here] = inv
        if p > 0:
            linv[here, 0 : p * CB] = -jnp.dot(
                inv, across, precision=HIGHEST, preferred_element_type=jnp.float32
            )
    for u in range(late, chunks + slots):
        arrive(u)
    for u in range(chunks + slots):
        finish(u)

    @pl.when(r == 0)
    def _():
        for d in range(1, n_row):
            ridge_copy(d).wait_send()


def schur_kernel(
    shape, n_row, n_col, place, rows, buf, linv, ridge, schur, panel, fh, fl, lh, ll, ch, cl
):
    width, depth, slots, per_tile = shape
    r = place[0]
    q = place[1]
    i = pl.program_id(0)
    step_rows = rows.shape[0]
    n_cols = slots * CB

    @pl.when(i == 0)
    def _():
        h, l = split(buf[...])
        fh[...] = h
        fl[...] = l
        h, l = split(linv[...])
        lh[...] = h
        ll[...] = l
        for s in range(slots):
            mine = slice(width + s * CB, width + (s + 1) * CB)
            k = kernel_value(
                dot3_t((fh[mine, :], fl[mine, :]), (fh[0:width, :], fl[0:width, :])), depth
            )
            first = (s * n_col + q) * CB
            delta = lax.broadcasted_iota(jnp.int32, k.shape, 1) - lax.broadcasted_iota(
                jnp.int32, k.shape, 0
            )
            k = k + jnp.where(delta == first, ridge[ridge.shape[0] - 1], 0.0)
            h, l = split(dot3_t(split(k), (lh[...], ll[...])))
            ch[s * CB : (s + 1) * CB, :] = h
            cl[s * CB : (s + 1) * CB, :] = l

    x = split(rows[...])
    t = i // per_tile
    first = (t * n_row + r) * width + (i % per_tile) * step_rows
    k = kernel_value(dot3_t(x, (fh[0:width, :], fl[0:width, :])), depth)
    delta = lax.broadcasted_iota(jnp.int32, k.shape, 1) - lax.broadcasted_iota(
        jnp.int32, k.shape, 0
    )
    k = k + jnp.where(delta == first, ridge[ridge.shape[0] - 1], 0.0)
    low = dot3_t(split(k), (lh[...], ll[...]))
    panel[...] = low
    low = split(low)
    delta = lax.broadcasted_iota(jnp.int32, (step_rows, CB), 0) - lax.broadcasted_iota(
        jnp.int32, (step_rows, CB), 1
    )
    wide = 2 if slots % 2 == 0 else 1
    for s0 in range(0, slots, wide):
        mine = slice(width + s0 * CB, width + (s0 + wide) * CB)
        these = slice(s0 * CB, (s0 + wide) * CB)
        value = kernel_value(dot3_t(x, (fh[mine, :], fl[mine, :])), depth) - dot3_t(
            low, (ch[these, :], cl[these, :])
        )
        for w in range(wide):
            s = s0 + w
            col = (s * n_col + q) * CB
            off = pl.multiple_of(col % width, CB)
            extra = jnp.where(delta == col - first, ridge[t, :, pl.ds(off, CB)], 0.0)
            part = value[:, w * CB : (w + 1) * CB] + extra
            if slots == 1:
                schur[...] = part
            else:
                schur[pl.ds(s, step_rows, stride=slots), :] = part


def per_device(features, ridge):
    tiles, _, width, depth = features.shape
    n_row = lax.axis_size("row")
    n_col = lax.axis_size("col")
    slots = tiles * n_row * width // (n_col * CB)
    chunks = width // CB
    units = chunks + slots
    feat = features.reshape(tiles, width, depth)
    ridge_rows = ridge.reshape(tiles, width)
    vmem = pl.BlockSpec(memory_space=pltpu.VMEM)
    linv, buf, ridge_p = pl.pallas_call(
        functools.partial(factor_kernel, (width, depth, chunks, slots), n_row, n_col),
        out_shape=(
            jax.ShapeDtypeStruct((width, width), jnp.float32),
            jax.ShapeDtypeStruct((units * CB, depth), jnp.float32),
            jax.ShapeDtypeStruct((1, width), jnp.float32),
        ),
        in_specs=[pl.BlockSpec(memory_space=pl.ANY), vmem],
        out_specs=(vmem, vmem, vmem),
        scratch_shapes=[
            pltpu.VMEM((2, CB, width), jnp.float32),
            pltpu.SemaphoreType.DMA((units,)),
            pltpu.SemaphoreType.DMA((units, n_row // 2)),
            pltpu.SemaphoreType.DMA((units,)),
            pltpu.SemaphoreType.DMA((units,)),
            pltpu.SemaphoreType.DMA((n_row,)),
            pltpu.SemaphoreType.DMA,
        ],
        compiler_params=pltpu.CompilerParams(
            collective_id=0, has_side_effects=True, vmem_limit_bytes=40 * 2**20
        ),
    )(feat, ridge_rows[0:1])

    place = jnp.stack([lax.axis_index("row"), lax.axis_index("col")])
    ridges = jnp.concatenate([ridge_rows, ridge_p], axis=0)[:, None, :]
    step_rows = 256
    per_tile = width // step_rows
    whole = lambda shape: pl.BlockSpec(shape, lambda i, place: (0,) * len(shape))
    schur, panel = pl.pallas_call(
        functools.partial(schur_kernel, (width, depth, slots, per_tile), n_row, n_col),
        out_shape=(
            jax.ShapeDtypeStruct((tiles * width * slots, CB), jnp.float32),
            jax.ShapeDtypeStruct((tiles * width, width), jnp.float32),
        ),
        grid_spec=pltpu.PrefetchScalarGridSpec(
            num_scalar_prefetch=1,
            grid=(tiles * per_tile,),
            in_specs=[
                pl.BlockSpec((step_rows, depth), lambda i, place: (i, 0)),
                whole((units * CB, depth)),
                whole((width, width)),
                whole((tiles + 1, 1, width)),
            ],
            out_specs=[
                pl.BlockSpec((step_rows * slots, CB), lambda i, place: (i, 0)),
                pl.BlockSpec((step_rows, width), lambda i, place: (i, 0)),
            ],
            scratch_shapes=[
                pltpu.VMEM((units * CB, depth), jnp.bfloat16),
                pltpu.VMEM((units * CB, depth), jnp.bfloat16),
                pltpu.VMEM((width, width), jnp.bfloat16),
                pltpu.VMEM((width, width), jnp.bfloat16),
                pltpu.VMEM((slots * CB, width), jnp.bfloat16),
                pltpu.VMEM((slots * CB, width), jnp.bfloat16),
            ],
        ),
        compiler_params=pltpu.CompilerParams(vmem_limit_bytes=48 * 2**20),
    )(place, features.reshape(tiles * width, depth), buf, linv, ridges)
    return (
        schur.reshape(tiles, 1, width, slots, 1, CB),
        panel.reshape(tiles, 1, width, width),
    )


def solution(mesh):
    in_specs = (P(None, "row", None, None), P(None, "row", None))
    out_specs = (P(None, "row", None, None, "col", None), P(None, "row", None, None))
    return jax.shard_map(
        per_device, mesh=mesh, in_specs=in_specs, out_specs=out_specs, check_vma=False
    )
```

```python
import functools

import jax
import jax.numpy as jnp
from jax import lax
from jax.experimental import pallas as pl
from jax.experimental.pallas import tpu as pltpu
from jax.sharding import PartitionSpec as P

CB = 128
STEP = 8
HIGHEST = lax.Precision.HIGHEST
MESH = pl.DeviceIdType.MESH


def dot_t(a, b, precision=None):
    return lax.dot_general(
        a, b, (((1,), (1,)), ((), ())), precision=precision, preferred_element_type=jnp.float32
    )


def split(x):
    hi = x.astype(jnp.bfloat16)
    return hi, (x - hi.astype(jnp.float32)).astype(jnp.bfloat16)


def dot3(a, b):
    return jnp.dot(
        jnp.concatenate([a[0], a[0], a[1]], axis=1),
        jnp.concatenate([b[0], b[1], b[0]], axis=0),
        preferred_element_type=jnp.float32,
    )


def kernel_value(inner, width):
    return jnp.square(inner * (1.0 / width) + 1.0)


def factor_inverse(w, midway):
    n = w.shape[0]
    lanes = lax.broadcasted_iota(jnp.int32, (1, n), 1)
    rows_out = []
    for j in range(0, n, STEP):
        if j == n // 2:
            midway()
        top = j // 8 * 8
        if w.shape[0] != n - top:
            w = w[8:, :]
        at = j - top
        ids = top + lax.broadcasted_iota(jnp.int32, w.shape, 0)
        all_lanes = lax.broadcasted_iota(jnp.int32, w.shape, 1)
        cols = [jnp.broadcast_to(w[:, j + k : j + k + 1], w.shape) for k in range(STEP)]
        inside = (all_lanes >= j) & (all_lanes < j + STEP) & (ids >= j)
        w = jnp.where(inside, jnp.where(ids == all_lanes, 1.0, 0.0), w)
        rows = [w[at + k : at + k + 1, :] for k in range(STEP)]
        for k in range(STEP):
            piv = cols[k][at + k : at + k + 1, :]
            inv = 1.0 / piv
            scaled = rows[k] * inv
            for m in range(k + 1, STEP):
                rows[m] = rows[m] - cols[k][at + m : at + m + 1, :] * scaled
                cols[m] = cols[m] - cols[k] * (cols[m][at + k : at + k + 1, :] * inv)
            w = w - jnp.where(ids > j + k, cols[k], 0.0) * scaled
            rows_out.append(jnp.where(lanes <= j + k, rows[k] * lax.rsqrt(piv), 0.0))
    return jnp.concatenate(rows_out, axis=0)


def factor_kernel(
    shape, n_row, n_col, feat, ridge0, linv, buf, ridge_p, kp_s,
    local_sem, send_sem, relay_sem, recv_sem, ridge_send, ridge_recv,
):
    width, depth, chunks, slots = shape
    r = lax.axis_index("row")
    q = lax.axis_index("col")
    mate = r + 1 - 2 * (r % 2)
    parity = r % 2
    pair = r // 2
    n_pair = n_row // 2

    barrier = pltpu.get_barrier_semaphore()
    for d in range(1, n_row):
        pl.semaphore_signal(
            barrier, inc=1, device_id=(lax.rem(r + d, n_row), q), device_id_type=MESH
        )
    pl.semaphore_wait(barrier, n_row - 1)

    def place(u):
        if u < chunks:
            return 0, 0, u * CB
        first = ((u - chunks) * n_col + q) * CB
        tile = first // width
        return tile % n_row, tile // n_row, first % width

    def source(u):
        owner, tile, off = place(u)
        return feat.at[tile, pl.ds(pl.multiple_of(off, CB), CB), :]

    def dest(u):
        return buf.at[pl.ds(u * CB, CB), :]

    def send(u, d):
        to = mate if d == 0 else 2 * lax.rem(pair + d, n_pair) + parity
        return pltpu.make_async_remote_copy(
            src_ref=source(u), dst_ref=dest(u), send_sem=send_sem.at[u, d],
            recv_sem=recv_sem.at[u], device_id=(to, q), device_id_type=MESH,
        )

    def forward(u):
        return pltpu.make_async_remote_copy(
            src_ref=dest(u), dst_ref=dest(u), send_sem=relay_sem.at[u],
            recv_sem=recv_sem.at[u], device_id=(mate, q), device_id_type=MESH,
        )

    def own(u):
        return pltpu.make_async_copy(source(u), dest(u), local_sem.at[u])

    def start(u):
        @pl.when(place(u)[0] == r)
        def _():
            for d in range(1, n_pair):
                send(u, d).start()
            send(u, 0).start()
            own(u).start()

    def is_relay(u):
        owner = place(u)[0]
        return (owner != r) & (owner % 2 == parity)

    def arrive(u):
        @pl.when(place(u)[0] == r)
        def _():
            own(u).wait()

        @pl.when(place(u)[0] != r)
        def _():
            forward(u).wait_recv()

        @pl.when(is_relay(u))
        def _():
            forward(u).start()

    def finish(u):
        @pl.when(place(u)[0] == r)
        def _():
            for d in range(n_pair):
                send(u, d).wait_send()

        @pl.when(is_relay(u))
        def _():
            forward(u).wait_send()

    def ridge_copy(d):
        return pltpu.make_async_remote_copy(
            src_ref=ridge0, dst_ref=ridge_p, send_sem=ridge_send.at[d], recv_sem=ridge_recv,
            device_id=(lax.rem(r + d, n_row), q), device_id_type=MESH,
        )

    @pl.when(r == 0)
    def _():
        for d in range(1, n_row):
            ridge_copy(d).start()
        ridge_p[...] = ridge0[...]

    for u in range(chunks):
        start(u)

    @pl.when(r != 0)
    def _():
        ridge_copy(1).wait_recv()

    linv[...] = jnp.zeros_like(linv)

    def arrive_cols():
        for u in range(chunks, chunks + slots):
            arrive(u)

    for p in range(chunks):
        arrive(p)
        if p == min(1, chunks - 1):
            for u in range(chunks, chunks + slots):
                start(u)
        here = slice(p * CB, (p + 1) * CB)
        upto = (p + 1) * CB
        mine = buf[here, :]
        for c in range(p + 1):
            there = slice(c * CB, (c + 1) * CB)
            kp_s[p % 2, :, there] = kernel_value(dot_t(mine, buf[there, :], HIGHEST), depth)
        eye = lax.broadcasted_iota(jnp.int32, (CB, CB), 0) == lax.broadcasted_iota(
            jnp.int32, (CB, CB), 1
        )
        s = kp_s[p % 2, :, here] + jnp.where(eye, ridge_p[:, here], 0.0)
        if p > 0:
            before = linv[0 : p * CB, 0 : p * CB]
            low = dot_t(kp_s[p % 2, :, 0 : p * CB], before, HIGHEST)
            s = s - dot_t(low, low, HIGHEST)
            across = jnp.dot(low, before, precision=HIGHEST, preferred_element_type=jnp.float32)
        inv = factor_inverse(s, arrive_cols if p == chunks - 1 else lambda: None)
        linv[here, here] = inv
        if p > 0:
            linv[here, 0 : p * CB] = -jnp.dot(
                inv, across, precision=HIGHEST, preferred_element_type=jnp.float32
            )
    for u in range(chunks + slots):
        finish(u)

    @pl.when(r == 0)
    def _():
        for d in range(1, n_row):
            ridge_copy(d).wait_send()


def schur_kernel(
    shape, n_row, n_col, place, rows, buf, linv, ridge, schur, panel, fh, fl, lh, ll, ch, cl
):
    width, depth, slots, per_tile = shape
    r = place[0]
    q = place[1]
    i = pl.program_id(0)
    step_rows = rows.shape[0]
    wide = 2 if slots % 2 == 0 else 1

    @pl.when(i == 0)
    def _():
        h, l = split(buf[...].T)
        fh[...] = h
        fl[...] = l
        h, l = split(linv[...].T)
        lh[...] = h
        ll[...] = l
        low_inv = split(linv[...])
        lead = split(buf[0:width, :])
        delta = lax.broadcasted_iota(jnp.int32, (width, CB), 0) - lax.broadcasted_iota(
            jnp.int32, (width, CB), 1
        )
        for s0 in range(0, slots, wide):
            mine = slice(width + s0 * CB, width + (s0 + wide) * CB)
            k = kernel_value(dot3(lead, (fh[:, mine], fl[:, mine])), depth)
            parts = []
            for w in range(wide):
                col = ((s0 + w) * n_col + q) * CB
                off = pl.multiple_of(col % width, CB)
                extra = jnp.where(delta == col, ridge[ridge.shape[0] - 1, :, pl.ds(off, CB)], 0.0)
                parts.append(k[:, w * CB : (w + 1) * CB] + extra)
            h, l = split(dot3(low_inv, split(jnp.concatenate(parts, axis=1))))
            ch[:, s0 * CB : (s0 + wide) * CB] = h
            cl[:, s0 * CB : (s0 + wide) * CB] = l

    x = split(rows[...])
    t = i // per_tile
    first = (t * n_row + r) * width + (i % per_tile) * step_rows
    k = kernel_value(dot3(x, (fh[:, 0:width], fl[:, 0:width])), depth)
    delta = lax.broadcasted_iota(jnp.int32, k.shape, 1) - lax.broadcasted_iota(
        jnp.int32, k.shape, 0
    )
    k = k + jnp.where(delta == first, ridge[ridge.shape[0] - 1], 0.0)
    low = dot3(split(k), (lh[...], ll[...]))
    panel[...] = low
    low = split(low)
    delta = lax.broadcasted_iota(jnp.int32, (step_rows, CB), 0) - lax.broadcasted_iota(
        jnp.int32, (step_rows, CB), 1
    )
    for s0 in range(0, slots, wide):
        mine = slice(width + s0 * CB, width + (s0 + wide) * CB)
        these = slice(s0 * CB, (s0 + wide) * CB)
        value = kernel_value(dot3(x, (fh[:, mine], fl[:, mine])), depth) - dot3(
            low, (ch[:, these], cl[:, these])
        )
        for w in range(wide):
            s = s0 + w
            col = (s * n_col + q) * CB
            off = pl.multiple_of(col % width, CB)
            extra = jnp.where(delta == col - first, ridge[t, :, pl.ds(off, CB)], 0.0)
            part = value[:, w * CB : (w + 1) * CB] + extra
            if slots == 1:
                schur[...] = part
            else:
                schur[pl.ds(s, step_rows, stride=slots), :] = part


def per_device(features, ridge):
    tiles, _, width, depth = features.shape
    n_row = lax.axis_size("row")
    n_col = lax.axis_size("col")
    slots = tiles * n_row * width // (n_col * CB)
    chunks = width // CB
    units = chunks + slots
    feat = features.reshape(tiles, width, depth)
    ridge_rows = ridge.reshape(tiles, width)
    vmem = pl.BlockSpec(memory_space=pltpu.VMEM)
    linv, buf, ridge_p = pl.pallas_call(
        functools.partial(factor_kernel, (width, depth, chunks, slots), n_row, n_col),
        out_shape=(
            jax.ShapeDtypeStruct((width, width), jnp.float32),
            jax.ShapeDtypeStruct((units * CB, depth), jnp.float32),
            jax.ShapeDtypeStruct((1, width), jnp.float32),
        ),
        in_specs=[pl.BlockSpec(memory_space=pl.ANY), vmem],
        out_specs=(vmem, vmem, vmem),
        scratch_shapes=[
            pltpu.VMEM((2, CB, width), jnp.float32),
            pltpu.SemaphoreType.DMA((units,)),
            pltpu.SemaphoreType.DMA((units, n_row // 2)),
            pltpu.SemaphoreType.DMA((units,)),
            pltpu.SemaphoreType.DMA((units,)),
            pltpu.SemaphoreType.DMA((n_row,)),
            pltpu.SemaphoreType.DMA,
        ],
        compiler_params=pltpu.CompilerParams(
            collective_id=0, has_side_effects=True, vmem_limit_bytes=40 * 2**20
        ),
    )(feat, ridge_rows[0:1])

    place = jnp.stack([lax.axis_index("row"), lax.axis_index("col")])
    ridges = jnp.concatenate([ridge_rows, ridge_p], axis=0)[:, None, :]
    step_rows = 256
    per_tile = width // step_rows
    whole = lambda shape: pl.BlockSpec(shape, lambda i, place: (0,) * len(shape))
    schur, panel = pl.pallas_call(
        functools.partial(schur_kernel, (width, depth, slots, per_tile), n_row, n_col),
        out_shape=(
            jax.ShapeDtypeStruct((tiles * width * slots, CB), jnp.float32),
            jax.ShapeDtypeStruct((tiles * width, width), jnp.float32),
        ),
        grid_spec=pltpu.PrefetchScalarGridSpec(
            num_scalar_prefetch=1,
            grid=(tiles * per_tile,),
            in_specs=[
                pl.BlockSpec((step_rows, depth), lambda i, place: (i, 0)),
                whole((units * CB, depth)),
                whole((width, width)),
                whole((tiles + 1, 1, width)),
            ],
            out_specs=[
                pl.BlockSpec((step_rows * slots, CB), lambda i, place: (i, 0)),
                pl.BlockSpec((step_rows, width), lambda i, place: (i, 0)),
            ],
            scratch_shapes=[
                pltpu.VMEM((depth, units * CB), jnp.bfloat16),
                pltpu.VMEM((depth, units * CB), jnp.bfloat16),
                pltpu.VMEM((width, width), jnp.bfloat16),
                pltpu.VMEM((width, width), jnp.bfloat16),
                pltpu.VMEM((width, slots * CB), jnp.bfloat16),
                pltpu.VMEM((width, slots * CB), jnp.bfloat16),
            ],
        ),
        compiler_params=pltpu.CompilerParams(vmem_limit_bytes=48 * 2**20),
    )(place, features.reshape(tiles * width, depth), buf, linv, ridges)
    return (
        schur.reshape(tiles, 1, width, slots, 1, CB),
        panel.reshape(tiles, 1, width, width),
    )


def solution(mesh):
    in_specs = (P(None, "row", None, None), P(None, "row", None))
    out_specs = (P(None, "row", None, None, "col", None), P(None, "row", None, None))
    return jax.shard_map(
        per_device, mesh=mesh, in_specs=in_specs, out_specs=out_specs, check_vma=False
    )
```
